256 devices in a mesh: dp: 16 (over y, z_hi, core), seq: 16 (over x, z_lo).
Axes of the slice: x: 4, y: 4, z: 8 (z_hi: 2, z_lo: 4; z = z_hi * 4 + z_lo), core: 2. Of those that a mesh axis runs over, the one named last changes fastest.
Arguments:
- query: bfloat16 [16, 2048, 6144], P('dp', 'seq')
- latent: bfloat16 [16, 2048, 512], P('dp', 'seq'), may hold values from -6 to 6
- rope_key: bfloat16 [16, 2048, 64], P('dp', 'seq')
- grad_mantissa: bfloat16 [16, 2048, 4096], P('dp', 'seq'), may hold values from -6 to 6
- grad_exponent: int32 [16, 2048, 32], P('dp', 'seq'), may hold values from -3 to 3
- forward_out: bfloat16 [16, 2048, 4096], P('dp', 'seq'), may hold values from -6 to 6
- offsets: int32 [16], P('dp'), may hold values from 0 to 1023
- w_key: bfloat16 [512, 32, 128], P(None, 'seq'), may hold values from -0.25 to 0.25
- w_value: bfloat16 [512, 32, 128], P(None, 'seq'), may hold values from -0.25 to 0.25
Outputs:
- grad_query: bfloat16 [16, 2048, 6144], P('dp', 'seq')
- grad_latent: float32 [16, 2048, 512], P('dp', 'seq')
- grad_rope: float32 [16, 2048, 64], P('dp', 'seq')
- grad_w_key: float32 [512, 32, 128], P(None, 'seq')
- grad_w_value: float32 [512, 32, 128], P(None, 'seq')
The draws below stay inside these ranges and needn't reach their ends.
Inputs may be any that keep to these rules, and one draw needn't show every extreme that they name: `grad_exponent`: the output gradient of one token and head is its 128 mantissa entries times 2 to this power. `offsets`: tokens before the offset are left padding; each of them attends only to itself.
All inputs are finite; a program needn't handle non-finite values.
Results may differ from the reference program's by a relative error of at most 0.02.
Values may be sent and summed in bfloat16 or wider, within the bound.
No kernel may reach another device: no remote copies, remote signals or barrier semaphores. Data moves between devices by JAX's collectives and lax.ppermute only.
A program may use at most 128 MiB of HBM per device.

```python
import jax
import jax.numpy as jnp
from jax import lax

LATENT = 512
ROPE = 64
NOPE = 128
VDIM = 128
HEADS = 32
SEQ_LEN = 2048
BATCH = 16
QK = 192


def rope_base(key):
    base = jax.random.normal(jax.random.fold_in(key, 11), (BATCH, SEQ_LEN, ROPE), jnp.float32)
    return jnp.clip(base, -4.0, 4.0)


def draw_rope_key(key, part):
    base = rope_base(key)
    return base.astype(jnp.bfloat16)


def draw_query(key, part):
    key = jax.random.fold_in(key, 5)
    values = jnp.clip(jax.random.normal(key, (BATCH, SEQ_LEN, HEADS, QK), jnp.float32), -5.0, 5.0)
    return values.reshape(BATCH, SEQ_LEN, HEADS * QK).astype(jnp.bfloat16)


def place_ends(result, rng, low, largest):
    longest = result.shape.index(max(result.shape))
    spots = []
    for shift in (0, 1):
        where = [jax.random.randint(jax.random.fold_in(rng, axis), (), 0, length) for axis, length in enumerate(result.shape)]
        where[longest] = (where[longest] + shift) % result.shape[longest]
        spots.append(tuple(where))
    return result.at[spots[0]].set(low).at[spots[1]].set(largest)


def shard_levels(own_key, shape, cuts, low, top_value):
    gain, own = 1.0, jax.random.fold_in(own_key, 6)
    for axis_at, parts in cuts:
        steps = jnp.exp(jax.random.uniform(jax.random.fold_in(own, axis_at), (parts,), jnp.float32, low / len(cuts), top_value / len(cuts)))
        gain = gain * jnp.repeat(steps, shape[axis_at] // parts).reshape([-1 if axis == axis_at else 1 for axis in range(len(shape))])
    return gain


def noise(own_key, shape, spread, bound, cuts=(), held_as=jnp.bfloat16):
    loudness = shard_levels(own_key, shape, cuts, -0.22, 0.18) if cuts else 1.0
    entries = jax.random.normal(own_key, shape, jnp.float32) * spread * loudness
    return jnp.minimum(jnp.maximum(entries, -bound), bound).astype(held_as)


def setup_inputs(seed: int = 0) -> dict:
    seeds = jax.random.split(jax.random.key(seed), 10)
    return {
        "query": draw_query(jax.random.fold_in(seeds[9], 71), 0),
        "latent": noise(seeds[1], (BATCH, SEQ_LEN, LATENT), 1.0, 6.0, ((0, 16), (1, 16))),
        "rope_key": draw_rope_key(jax.random.fold_in(seeds[9], 71), 0),
        "grad_mantissa": noise(seeds[3], (BATCH, SEQ_LEN, HEADS * VDIM), 1.0, 6.0, ((0, 16), (1, 16))),
        "grad_exponent": place_ends(jax.random.randint(seeds[4], (BATCH, SEQ_LEN, HEADS), -3, 4), jax.random.fold_in(seeds[4], 1), -3, 3).astype(jnp.int32),
        "forward_out": noise(seeds[5], (BATCH, SEQ_LEN, HEADS * VDIM), 1.0, 6.0, ((0, 16), (1, 16))),
        "offsets": place_ends(jax.random.randint(seeds[6], (BATCH,), 0, SEQ_LEN // 2), jax.random.fold_in(seeds[6], 1), 0, (SEQ_LEN // 2) - 1).astype(jnp.int32),
        "w_key": noise(seeds[7], (LATENT, HEADS, NOPE), LATENT ** -0.5, 0.25, ((1, 16),)),
        "w_value": noise(seeds[8], (LATENT, HEADS, VDIM), LATENT ** -0.5, 0.25, ((1, 16),)),
    }


def sequence_grads(query_seq, latent_seq, rope_seq, mantissa_seq, exponent_seq, saved_seq, offset, key_weights, value_weights):
    score_scale = QK ** -0.5
    scaled = mantissa_seq.reshape(SEQ_LEN, HEADS, VDIM).astype(jnp.float32) * jnp.exp2(exponent_seq.astype(jnp.float32))[:, :, None]
    dout = scaled.astype(jnp.bfloat16)
    query_heads = query_seq.reshape(SEQ_LEN, HEADS, QK).transpose(1, 0, 2)
    dout_heads = dout.transpose(1, 0, 2)
    saved_heads = saved_seq.reshape(SEQ_LEN, HEADS, VDIM).transpose(1, 0, 2)
    positions = jnp.arange(SEQ_LEN, dtype=jnp.int32)
    visible = ((positions[None, :] <= positions[:, None]) & (positions[None, :] >= offset)) | (positions[None, :] == positions[:, None])

    def per_head(carry, pieces):
        latent_sum, rope_sum = carry
        query_head, dout_head, saved_head, key_weight, value_weight = pieces
        key_nope = jnp.dot(latent_seq, key_weight, preferred_element_type=jnp.float32).astype(jnp.bfloat16)
        value_rows = jnp.dot(latent_seq, value_weight, preferred_element_type=jnp.float32).astype(jnp.bfloat16)
        key_rows = jnp.concatenate([key_nope, rope_seq], axis=1)
        scores = jnp.dot(query_head, key_rows.T, preferred_element_type=jnp.float32) * score_scale
        scores = jnp.where(visible, scores, jnp.float32(-1e30))
        row_peak = jnp.max(scores, axis=1, keepdims=True)
        expo_terms = jnp.exp(scores - row_peak)
        attn_probs = expo_terms / jnp.sum(expo_terms, axis=1, keepdims=True)
        row_delta = jnp.sum(dout_head.astype(jnp.float32) * saved_head.astype(jnp.float32), axis=1)
        dprob = jnp.dot(dout_head, value_rows.T, preferred_element_type=jnp.float32)
        dscore = attn_probs * (dprob - row_delta[:, None])
        probs_low = attn_probs.astype(jnp.bfloat16)
        dscore_low = dscore.astype(jnp.bfloat16)
        grad_value = jnp.dot(probs_low.T, dout_head, preferred_element_type=jnp.float32).astype(jnp.bfloat16)
        grad_query = (jnp.dot(dscore_low, key_rows, preferred_element_type=jnp.float32) * score_scale).astype(jnp.bfloat16)
        grad_key = jnp.dot(dscore_low.T, query_head, preferred_element_type=jnp.float32) * score_scale
        grad_nope = grad_key[:, :NOPE].astype(jnp.bfloat16)
        latent_term = jnp.dot(grad_nope, key_weight.T, preferred_element_type=jnp.float32) + jnp.dot(grad_value, value_weight.T, preferred_element_type=jnp.float32)
        weight_key = jnp.dot(latent_seq.T, grad_nope, preferred_element_type=jnp.float32)
        weight_value = jnp.dot(latent_seq.T, grad_value, preferred_element_type=jnp.float32)
        return (latent_sum + latent_term, rope_sum + grad_key[:, NOPE:]), (grad_query, weight_key, weight_value)

    start_carry = (jnp.zeros((SEQ_LEN, LATENT), jnp.float32), jnp.zeros((SEQ_LEN, ROPE), jnp.float32))
    pieces = (query_heads, dout_heads, saved_heads, key_weights.transpose(1, 0, 2), value_weights.transpose(1, 0, 2))
    (latent_sum, rope_sum), (grad_query, weight_key, weight_value) = lax.scan(per_head, start_carry, pieces)
    grad_query = grad_query.transpose(1, 0, 2).reshape(SEQ_LEN, HEADS * QK)
    return grad_query, latent_sum, rope_sum, weight_key, weight_value


def reference(query, latent, rope_key, grad_mantissa, grad_exponent, forward_out, offsets, w_key, w_value):
    def per_sequence(carry, pieces):
        key_total, value_total = carry
        query_seq, latent_seq, rope_seq, mantissa_seq, exponent_seq, saved_seq, offset = pieces
        grad_query, latent_sum, rope_sum, weight_key, weight_value = sequence_grads(query_seq, latent_seq, rope_seq, mantissa_seq, exponent_seq, saved_seq, offset, w_key, w_value)
        return (key_total + weight_key, value_total + weight_value), (grad_query, latent_sum, rope_sum)

    start_carry = (jnp.zeros((HEADS, LATENT, NOPE), jnp.float32), jnp.zeros((HEADS, LATENT, VDIM), jnp.float32))
    pieces = (query, latent, rope_key, grad_mantissa, grad_exponent, forward_out, offsets)
    (key_total, value_total), (grad_query, grad_latent, grad_rope) = lax.scan(per_sequence, start_carry, pieces)
    return grad_query, grad_latent, grad_rope, key_total.transpose(1, 0, 2), value_total.transpose(1, 0, 2)
```

```python
import functools

import jax
import jax.numpy as jnp
import numpy as np
from jax import lax
from jax.experimental import pallas as pl
from jax.experimental.pallas import tpu as pltpu
from jax.sharding import PartitionSpec as P

LATENT = 512
ROPE = 64
NOPE = 128
VDIM = 128
QK = NOPE + ROPE
TOK = 128
PAIR = 2 * QK
MSG = PAIR + 2 * VDIM
SCALE = QK ** (-0.5)
LOG2E = 1.4426950408889634
BIG = -1e30
NY, NZH, NC, NX, NZ = 4, 2, 2, 4, 4
BF, F32 = jnp.bfloat16, jnp.float32


def dot(a, b):
    return jnp.dot(a, b, preferred_element_type=F32)


def moves(dy=0, dc=0, dx=0, dz=0, ring=0):
    pairs = []
    for index in np.ndindex(NY, NZH, NC, NX, NZ):
        y, zh, c, x, z = index
        along = (zh * NZ + z + ring) % (NZH * NZ)
        zh2, z2 = along // NZ, (along % NZ + dz) % NZ
        dest = ((y + dy) % NY, zh2, (c + dc) % NC, (x + dx) % NX, z2)
        shape = (NY, NZH, NC, NX, NZ)
        pairs.append((int(np.ravel_multi_index(index, shape)), int(np.ravel_multi_index(dest, shape))))
    return pairs


def send(value, **shift):
    return lax.ppermute(value, ("dp", "seq"), moves(**shift))


def pack_kernel(first, sc, q0, q1, m0, m1, f0, f1, ex, *outs):
    step = pl.program_id(0)
    x, z = sc[0], sc[1]
    for kk, (q, m, f) in enumerate(((q0, m0, f0), (q1, m1, f1))):
        block = ((x + step) & 3) * NZ + ((z + first + kk) & 3)
        rows = pl.ds(kk * TOK, TOK)
        exps = ex[...]
        lane = lax.broadcasted_iota(jnp.int32, exps.shape, 1)
        grads, deltas = [], []
        for h in range(2):
            e = jnp.sum(jnp.where(lane == 2 * block + h, exps, 0), axis=1, keepdims=True)
            scale = jnp.left_shift(jnp.ones_like(e), e + 3).astype(F32) * 0.125
            part = slice(h * VDIM, (h + 1) * VDIM)
            g = (m[:, part].astype(F32) * scale).astype(BF)
            grads.append(g)
            prod = g.astype(F32) * f[:, part].astype(F32)
            d = jnp.sum(prod.T, axis=0, keepdims=True)
            hi = d.astype(BF).astype(F32)
            mid = (d - hi).astype(BF).astype(F32)
            row = lax.broadcasted_iota(jnp.int32, (16, TOK), 0)
            deltas.append(
                jnp.where(row == 0, hi, jnp.where(row == 1, mid, jnp.where(row == 2, d - hi - mid, 0.0)))
            )
        for s in range(4):

            @pl.when(step == s)
            def _():
                outs[s][rows, :PAIR] = q[...]
                outs[s][rows, PAIR : PAIR + VDIM] = grads[0]
                outs[s][rows, PAIR + VDIM :] = grads[1]
                outs[s][2 * TOK :, kk * 256 : kk * 256 + 256] = jnp.concatenate(deltas, axis=1).astype(BF)
                if kk == 0:
                    outs[s][2 * TOK :, 512:] = jnp.zeros((16, MSG - 512), BF)


def pack(first, sc, query, mantissa, exponent, saved):
    def at(kk):
        return lambda s, sc: (0, ((sc[0] + s) & 3) * NZ + ((sc[1] + first + kk) & 3))

    full = pl.BlockSpec((2 * TOK + 16, MSG), lambda s, sc: (0, 0))
    return pl.pallas_call(
        functools.partial(pack_kernel, first),
        grid_spec=pltpu.PrefetchScalarGridSpec(
            num_scalar_prefetch=1,
            grid=(4,),
            in_specs=[
                pl.BlockSpec((TOK, PAIR), at(0)),
                pl.BlockSpec((TOK, PAIR), at(1)),
                pl.BlockSpec((TOK, 256), at(0)),
                pl.BlockSpec((TOK, 256), at(1)),
                pl.BlockSpec((TOK, 256), at(0)),
                pl.BlockSpec((TOK, 256), at(1)),
                pl.BlockSpec((TOK, 32), lambda s, sc: (0, 0)),
            ],
            out_specs=[full] * 4,
        ),
        out_shape=[jax.ShapeDtypeStruct((2 * TOK + 16, MSG), BF)] * 4,
        cost_estimate=pl.CostEstimate(flops=2_000_000, bytes_accessed=4_000_000, transcendentals=0),
        name="pack",
    )(sc, query, query, mantissa, mantissa, saved, saved, exponent)


def attn_kernel(has_prior, sc, *refs):
    msgs, lats, (wa, wb) = refs[0:4], refs[4:8], refs[8:10]
    refs = refs[10:]
    priors = refs[:4] if has_prior else None
    refs = refs[4:] if has_prior else refs
    dqs, gls, (gkeep, gsend) = refs[0:4], refs[4:8], refs[8:10]
    lat, lat_t, kx, kx_t, acc, acc_r, w, w_t, kn, vs, qs, gs, dl, dkv, dq_scr, gw, s0, s1, s2, s3 = refs[10:]
    slabs = (s0, s1, s2, s3)
    kk = pl.program_id(0)
    x, z, off, core, y = sc[0], sc[1], sc[2], sc[3], sc[4]

    @pl.when(kk == 0)
    def _():
        for s in range(4):
            j = (x - s) & 3
            slab = lats[s][:, :LATENT]
            lat[j] = slab
            lat_t[j] = slab.T
            r = lax.broadcasted_iota(jnp.int32, (512, ROPE), 0)
            lane = lax.broadcasted_iota(jnp.int32, (512, ROPE), 1)
            blk = r >> 7
            pos = 512 * j + 128 * ((z - blk) & 3) + (r & 127)
            hide = ((lane == 0) & (pos < off)) | ((lane == 1 + j) & (blk > z))
            extra = jnp.where(hide, BIG, 0.0).astype(BF)
            both = jnp.concatenate([lats[s][:, LATENT:], extra], axis=1)
            kx[j] = both
            kx_t[j] = both.T
            i = (x + s) & 3
            if has_prior:
                acc[i] = priors[s][:, :LATENT].astype(F32)
                acc_r[i] = priors[s][:, LATENT:].astype(F32)
            else:
                acc[i] = jnp.zeros((512, LATENT), F32)
                acc_r[i] = jnp.zeros((512, ROPE), F32)
        w[...] = wa[...]

    @pl.when(kk == 1)
    def _():
        w[...] = wb[...]

    weights = w[...]
    w_t[...] = weights.T
    for j in range(4):
        kv = dot(lat[j], weights).astype(BF)
        for h in range(2):
            kn[h, j] = kv[:, h * 128 : h * 128 + 128]
            vs[h, j] = kv[:, 256 + h * 128 : 384 + h * 128]
    rows = pl.ds(pl.multiple_of(kk * TOK, TOK), TOK)
    for s in range(4):
        i = (x - s) & 3
        lane = lax.broadcasted_iota(jnp.int32, (TOK, ROPE), 1)
        ones = jnp.where((lane == 0) | (lane == 1 + i), 1.0, 0.0).astype(BF)
        for h in range(2):
            qs[h, i] = jnp.concatenate([msgs[s][rows, h * QK : h * QK + QK], ones], axis=1)
            gs[h, i] = msgs[s][rows, PAIR + h * VDIM : PAIR + (h + 1) * VDIM]
            lanes = pl.ds(pl.multiple_of((2 * kk + h) * TOK, TOK), TOK)
            part = jnp.sum(msgs[s][2 * TOK :, lanes].astype(F32), axis=0, keepdims=True)
            dl[h, i] = jnp.broadcast_to(part, (8, TOK))

    r = lax.broadcasted_iota(jnp.int32, (128, 128), 0)
    c = lax.broadcasted_iota(jnp.int32, (128, 128), 1)
    for h in range(2):
        q = qs[h].reshape(512, 256)
        q_t = q.T
        peaks = [None] * 4
        for j in range(4):
            keys = jnp.concatenate([kn[h, j], kx[j]], axis=1)
            sj = dot(keys, q_t[:, 128 * j :])
            pos = 512 * j + 128 * z + r
            own = jnp.where(r <= c, sj[:128, :128], BIG)
            own = jnp.where((r == c) & (pos < off), 0.0, own)
            slabs[j][:128, :128] = own
            if j < 3:
                slabs[j][:128, 128:] = sj[:128, 128:]
            slabs[j][128:, :] = sj[128:, :]
            top = jnp.max(sj[128:, :], axis=0, keepdims=True)
            head = jnp.max(own, axis=0, keepdims=True)
            if j < 3:
                head = jnp.concatenate([head, jnp.max(sj[:128, 128:], axis=0, keepdims=True)], axis=1)
            top = jnp.maximum(top, head)
            for i in range(j, 4):
                piece = top[:, 128 * (i - j) : 128 * (i - j) + 128]
                peaks[i] = piece if peaks[i] is None else jnp.maximum(peaks[i], piece)
        peak = jnp.concatenate(peaks, axis=1)
        total = jnp.zeros((1, 512), F32)
        for j in range(4):
            e = jnp.exp2((slabs[j][...] - peak[:, 128 * j :]) * (SCALE * LOG2E))
            slabs[j][...] = e
            add = jnp.sum(e, axis=0, keepdims=True)
            if j:
                add = jnp.concatenate([jnp.zeros((1, 128 * j), F32), add], axis=1)
            total = total + add
        inv = 1.0 / total
        g_t = gs[h].reshape(512, VDIM).T
        gn_t = (g_t.astype(F32) * inv).astype(BF)
        gn = gn_t.T
        delta = jnp.concatenate([dl[h, i][:1] for i in range(4)], axis=1) * inv
        dq_t = jnp.zeros((QK, 512), F32)
        for j in range(4):
            cut = slice(128 * j, 512)
            e = slabs[j][...]
            dp = dot(vs[h, j], gn_t[:, cut])
            ds = (e * (dp - delta[:, cut])).astype(BF)
            dv = dot(e.astype(BF), gn[cut])
            dk = dot(ds, q[cut]) * SCALE
            dkv[j, :, h * 128 : h * 128 + 128] = dk[:, :NOPE].astype(BF)
            dkv[j, :, 256 + h * 128 : 384 + h * 128] = dv.astype(BF)
            acc_r[j] += dk[:, NOPE:QK]
            keys_t = jnp.concatenate([kn[h, j].T, kx_t[j][:ROPE]], axis=0)
            add = dot(keys_t, ds)
            if j:
                add = jnp.concatenate([jnp.zeros((QK, 128 * j), F32), add], axis=1)
            dq_t = dq_t + add
        dq = (dq_t * SCALE).T.astype(BF)
        for i in range(4):
            dq_scr[(i - x) & 3, :, h * QK : h * QK + QK] = dq[128 * i : 128 * i + 128]

    total_w = None
    for j in range(4):
        both = dkv[j]
        acc[j] += dot(both, w_t[...])
        add = dot(lat_t[j], both)
        total_w = add if total_w is None else total_w + add
    gw[...] = total_w
    for s in range(4):
        dqs[s][...] = dq_scr[s]
        at = ((y + s) & 3) * 64
        gkeep[s, 0] = gw[pl.ds(pl.multiple_of(core * 256 + at, 64), 64), :].astype(BF)
        gsend[s, 0] = gw[pl.ds(pl.multiple_of((1 - core) * 256 + at, 64), 64), :].astype(BF)

    @pl.when(kk == 1)
    def _():
        for s in range(4):
            i = (x + s) & 3
            gls[s][:, :LATENT] = acc[i].astype(BF)
            gls[s][:, LATENT:] = acc_r[i].astype(BF)


def attention(sc, msgs, lats, wa, wb, priors):
    def whole(shape):
        return pl.BlockSpec(shape, lambda k, sc: (0,) * len(shape))

    has_prior = priors is not None
    slab = whole((512, LATENT + ROPE))
    in_specs = [whole((2 * TOK + 16, MSG))] * 4 + [slab] * 4 + [whole((512, 512))] * 2
    args = [*msgs, *lats, wa, wb]
    if has_prior:
        in_specs += [slab] * 4
        args += list(priors)
    out_specs = (
        [pl.BlockSpec((TOK, PAIR), lambda k, sc: (k, 0))] * 4
        + [slab] * 4
        + [pl.BlockSpec((4, 1, 64, 512), lambda k, sc: (0, k, 0, 0))] * 2
    )
    out_shape = (
        [jax.ShapeDtypeStruct((2 * TOK, PAIR), BF)] * 4
        + [jax.ShapeDtypeStruct((512, LATENT + ROPE), BF)] * 4
        + [jax.ShapeDtypeStruct((4, 2, 64, 512), BF)] * 2
    )
    scratch = [
        pltpu.VMEM((4, 512, LATENT), BF),
        pltpu.VMEM((4, LATENT, 512), BF),
        pltpu.VMEM((4, 512, 128), BF),
        pltpu.VMEM((4, 128, 512), BF),
        pltpu.VMEM((4, 512, LATENT), F32),
        pltpu.VMEM((4, 512, ROPE), F32),
        pltpu.VMEM((512, 512), BF),
        pltpu.VMEM((512, 512), BF),
        pltpu.VMEM((2, 4, 512, 128), BF),
        pltpu.VMEM((2, 4, 512, 128), BF),
        pltpu.VMEM((2, 4, TOK, 256), BF),
        pltpu.VMEM((2, 4, TOK, VDIM), BF),
        pltpu.VMEM((2, 4, 8, TOK), F32),
        pltpu.VMEM((4, 512, 512), BF),
        pltpu.VMEM((4, TOK, PAIR), BF),
        pltpu.VMEM((512, 512), F32),
        pltpu.VMEM((512, 512), F32),
        pltpu.VMEM((512, 384), F32),
        pltpu.VMEM((512, 256), F32),
        pltpu.VMEM((512, 128), F32),
    ]
    outs = pl.pallas_call(
        functools.partial(attn_kernel, has_prior),
        grid_spec=pltpu.PrefetchScalarGridSpec(
            num_scalar_prefetch=1, grid=(2,), in_specs=in_specs, out_specs=out_specs, scratch_shapes=scratch
        ),
        out_shape=out_shape,
        compiler_params=pltpu.CompilerParams(vmem_limit_bytes=56 * 1024 * 1024),
        cost_estimate=pl.CostEstimate(flops=25_000_000_000, bytes_accessed=10_000_000, transcendentals=2_700_000),
        name="attention",
    )(sc, *args)
    return outs[0:4], outs[4:8], outs[8], outs[9]


def unpack_kernel(sc, *refs):
    out = refs[8]
    x, z = sc[0], sc[1]
    for call in range(2):
        for s in range(4):
            for kk in range(2):
                block = ((x - s) & 3) * NZ + ((z + 2 * call + kk) & 3)
                lanes = pl.ds(pl.multiple_of(block * PAIR, 128), PAIR)
                out[:, lanes] = refs[call * 4 + s][kk * TOK : kk * TOK + TOK, :]


def unpack(sc, pieces):
    spec = pl.BlockSpec(memory_space=pltpu.VMEM)
    return pl.pallas_call(
        unpack_kernel,
        in_specs=[pl.BlockSpec(memory_space=pltpu.SMEM)] + [spec] * 8,
        out_specs=spec,
        out_shape=jax.ShapeDtypeStruct((TOK, 16 * PAIR), BF),
        cost_estimate=pl.CostEstimate(flops=0, bytes_accessed=3_000_000, transcendentals=0),
        name="unpack",
    )(sc, *pieces)


def weights_kernel(sc, *refs):
    mine, other, out_k, out_v = refs[:4], refs[4], refs[5], refs[6]
    core, y = sc[3], sc[4]
    for s in range(4):
        at = ((y - s) & 3) * 64
        for base, ref in ((core, mine[s][...]), (1 - core, other[s])):
            rows = pl.ds(pl.multiple_of(base * 256 + at, 64), 64)
            out_k[rows, :] = ref[:, :256].astype(F32)
            out_v[rows, :] = ref[:, 256:].astype(F32)


def place_weights(sc, mine, other):
    spec = pl.BlockSpec(memory_space=pltpu.VMEM)
    return pl.pallas_call(
        weights_kernel,
        in_specs=[pl.BlockSpec(memory_space=pltpu.SMEM)] + [spec] * 5,
        out_specs=[spec] * 2,
        out_shape=[jax.ShapeDtypeStruct((512, 256), F32)] * 2,
        cost_estimate=pl.CostEstimate(flops=0, bytes_accessed=2_000_000, transcendentals=0),
        name="place_weights",
    )(sc, *mine, other)


def summed(parts):
    total = parts[0].astype(F32)
    for part in parts[1:]:
        total = total + part.astype(F32)
    return total


def shards(query, latent, rope_key, grad_mantissa, grad_exponent, forward_out, offsets, w_key, w_value):
    dp, seq = lax.axis_index("dp"), lax.axis_index("seq")
    x, z = seq // NZ, seq % NZ
    y, core = dp // (NZH * NC), dp % NC
    sc = jnp.stack([x, z, offsets[0], core, y]).astype(jnp.int32)

    own = jnp.concatenate([latent[0], rope_key[0]], axis=1)
    slab = jnp.concatenate([own] + [send(own, dz=s) for s in (1, 2, 3)], axis=0)
    lats = [slab] + [send(slab, dx=s) for s in (1, 2, 3)]

    w_own = jnp.concatenate([w_key.reshape(LATENT, 256), w_value.reshape(LATENT, 256)], axis=1)
    w_all = [w_own, send(w_own, ring=-1), None, send(w_own, ring=1)]
    w_all[2] = jnp.concatenate([send(w_own[:256], ring=-2), send(w_own[256:], ring=2)], axis=0)

    arrived = []
    for first in (0, 2):
        out = pack(first, sc, query[0], grad_mantissa[0], grad_exponent[0], forward_out[0])
        arrived.append([out[0]] + [send(out[s], dx=s) for s in (1, 2, 3)])

    priors, pieces, partial = None, [], []
    for call in range(2):
        dqs, priors, keep, away = attention(
            sc, arrived[call], lats, w_all[2 * call], w_all[2 * call + 1], priors
        )
        pieces += [dqs[0]] + [send(dqs[s], dx=s) for s in (1, 2, 3)]
        both = (keep.astype(F32) + send(away, dc=1).astype(F32)).astype(BF)
        partial.append(summed([both[0]] + [send(both[s], dy=s) for s in (1, 2, 3)]).astype(BF))
    grad_query = unpack(sc, pieces)

    along_x = summed([priors[0]] + [send(priors[s], dx=s) for s in (1, 2, 3)]).astype(BF)
    blocks = along_x.reshape(NZ, TOK, LATENT + ROPE)
    along_z = summed([blocks[0]] + [send(blocks[s], dz=-s) for s in (1, 2, 3)])

    own_heads = summed(
        [
            partial[0][0],
            send(partial[0][1], ring=1),
            send(partial[1][0], ring=2),
            send(partial[1][1], ring=-1),
        ]
    ).astype(BF)
    own_heads = (own_heads.astype(F32) + send(own_heads, ring=4).astype(F32)).astype(BF)
    mine = [own_heads] + [send(own_heads, dy=s) for s in (1, 2, 3)]
    other = send(jnp.stack(mine), dc=1)
    total_key, total_value = place_weights(sc, mine, other)
    return (
        grad_query[None],
        along_z[None, :, :LATENT],
        along_z[None, :, LATENT:],
        total_key.reshape(LATENT, 2, NOPE),
        total_value.reshape(LATENT, 2, VDIM),
    )


def solution(mesh):
    tokens = P("dp", "seq", None)
    heads = P(None, "seq", None)
    in_specs = (tokens,) * 6 + (P("dp"), heads, heads)
    out_specs = (tokens,) * 3 + (heads, heads)
    return jax.shard_map(shards, mesh=mesh, in_specs=in_specs, out_specs=out_specs, check_vma=False)
```

```python
import functools

import jax
import jax.numpy as jnp
import numpy as np
from jax import lax
from jax.experimental import pallas as pl
from jax.experimental.pallas import tpu as pltpu
from jax.sharding import PartitionSpec as P

LATENT = 512
ROPE = 64
NOPE = 128
VDIM = 128
QK = NOPE + ROPE
TOK = 128
PAIR = 2 * QK
MSG = PAIR + 2 * VDIM
BLOCK = TOK + 16
SLAB = 4 * BLOCK
GROUPS = ((0, 1), (3, 2))
SCALE = QK ** (-0.5)
LOG2E = 1.4426950408889634
BIG = -1e30
NY, NZH, NC, NX, NZ = 4, 2, 2, 4, 4
BF, F32 = jnp.bfloat16, jnp.float32


def dot(a, b):
    return jnp.dot(a, b, preferred_element_type=F32)


def moves(dy=0, dc=0, dx=0, dz=0, ring=0):
    pairs = []
    shape = (NY, NZH, NC, NX, NZ)
    for index in np.ndindex(*shape):
        y, zh, c, x, z = index
        along = (zh * NZ + z + ring) % (NZH * NZ)
        dest = ((y + dy) % NY, along // NZ, (c + dc) % NC, (x + dx) % NX, (along + dz) % NZ)
        pairs.append((int(np.ravel_multi_index(index, shape)), int(np.ravel_multi_index(dest, shape))))
    return pairs


def send(value, **shift):
    return lax.ppermute(value, ("dp", "seq"), moves(**shift))


def trade(value, axis):
    groups = {
        "x": [[z + NZ * x for x in range(NX)] for z in range(NZ)],
        "z": [[z + NZ * x for z in range(NZ)] for x in range(NX)],
        "y": [[r + NZH * NC * y for y in range(NY)] for r in range(NZH * NC)],
    }[axis]
    return lax.all_to_all(value, "dp" if axis == "y" else "seq", 0, 0, axis_index_groups=groups)


def spread(value, axis):
    return trade(jnp.broadcast_to(value[None], (4, *value.shape)), axis)


def pack_kernel(groups, sc, q0, q1, m0, m1, f0, f1, ex, out):
    step = pl.program_id(0)
    for kk, (q, m, f) in enumerate(((q0, m0, f0), (q1, m1, f1))):
        rows = slice(kk * TOK, kk * TOK + TOK)
        exps = ex[...]
        lane = lax.broadcasted_iota(jnp.int32, exps.shape, 1)
        grads, deltas = [], []
        for h in range(2):
            e = jnp.sum(jnp.where(lane == 2 * (step * NZ + ((sc[0] + groups[kk]) & 3)) + h, exps, 0), axis=1, keepdims=True)
            scale = jnp.left_shift(jnp.ones_like(e), e + 3).astype(F32) * 0.125
            part = slice(h * VDIM, (h + 1) * VDIM)
            g = (m[:, part].astype(F32) * scale).astype(BF)
            grads.append(g)
            prod = g.astype(F32) * f[:, part].astype(F32)
            d = jnp.sum(prod.T, axis=0, keepdims=True)
            hi = d.astype(BF).astype(F32)
            mid = (d - hi).astype(BF).astype(F32)
            row = lax.broadcasted_iota(jnp.int32, (16, TOK), 0)
            deltas.append(
                jnp.where(row == 0, hi, jnp.where(row == 1, mid, jnp.where(row == 2, d - hi - mid, 0.0)))
            )
        out[0, rows, :PAIR] = q[...]
        out[0, rows, PAIR : PAIR + VDIM] = grads[0]
        out[0, rows, PAIR + VDIM :] = grads[1]
        out[0, 2 * TOK :, kk * 256 : kk * 256 + 256] = jnp.concatenate(deltas, axis=1).astype(BF)
    out[0, 2 * TOK :, 512:] = jnp.zeros((16, MSG - 512), BF)


def pack(groups, sc, query, mantissa, exponent, saved):
    def at(kk):
        return lambda s, sc: (0, s * NZ + ((sc[0] + groups[kk]) & 3))

    return pl.pallas_call(
        functools.partial(pack_kernel, groups),
        grid_spec=pltpu.PrefetchScalarGridSpec(
            num_scalar_prefetch=1,
            grid=(4,),
            in_specs=[
                pl.BlockSpec((TOK, PAIR), at(0)),
                pl.BlockSpec((TOK, PAIR), at(1)),
                pl.BlockSpec((TOK, 256), at(0)),
                pl.BlockSpec((TOK, 256), at(1)),
                pl.BlockSpec((TOK, 256), at(0)),
                pl.BlockSpec((TOK, 256), at(1)),
                pl.BlockSpec((TOK, 32), lambda s, sc: (0, 0)),
            ],
            out_specs=pl.BlockSpec((1, 2 * TOK + 16, MSG), lambda s, sc: (s, 0, 0)),
        ),
        out_shape=jax.ShapeDtypeStruct((4, 2 * TOK + 16, MSG), BF),
        cost_estimate=pl.CostEstimate(flops=2_000_000, bytes_accessed=4_000_000, transcendentals=0),
        name="pack",
    )(sc, query, query, mantissa, mantissa, saved, saved, exponent)


def attn_kernel(has_prior, sc, *refs):
    msgs, lats, given = refs[0], refs[1:5], refs[5:7]
    priors = refs[7:11]
    refs = refs[11:] if has_prior else refs[7:]
    dqs = refs[:4] if has_prior else refs[:1]
    refs = refs[len(dqs) :]
    gls, gkeep, gsend = refs[0:4], refs[4], refs[5]
    lat, lat_t, kx, kx_t, acc, acc_r, w, w_t, kn, vs, qs, gs, dl, dkv, dq_scr, gw, s0, s1, s2, s3 = refs[6:]
    slabs = (s0, s1, s2, s3)
    kk = pl.program_id(0)
    z, off, core, x, y = sc[0], sc[1], sc[2], sc[3], sc[4]

    @pl.when(kk == 0)
    def _():
        for s in range(4):
            j = (x - s) & 3
            ropes = []
            for b in range(4):
                block = lats[s][b * BLOCK : b * BLOCK + TOK, :]
                lat[j, b * TOK : b * TOK + TOK, :] = block
                lat_t[j, :, b * TOK : b * TOK + TOK] = block.T
                packed = lats[s][b * BLOCK + TOK : b * BLOCK + BLOCK, :]
                ropes += [packed[:, ROPE * c : ROPE * c + ROPE] for c in range(8)]
            r = lax.broadcasted_iota(jnp.int32, (512, ROPE), 0)
            lane = lax.broadcasted_iota(jnp.int32, (512, ROPE), 1)
            blk = r >> 7
            pos = 512 * j + 128 * ((z - blk) & 3) + (r & 127)
            hide = ((lane == 0) & (pos < off)) | ((lane == 1 + j) & (blk > z))
            extra = jnp.where(hide, BIG, 0.0).astype(BF)
            both = jnp.concatenate([jnp.concatenate(ropes, axis=0), extra], axis=1)
            kx[j] = both
            kx_t[j] = both.T
            i = (x + s) & 3
            if has_prior:
                for b in range(4):
                    acc[i, b * TOK : b * TOK + TOK, :] = priors[s][b * BLOCK : b * BLOCK + TOK, :].astype(F32)
                    packed = priors[s][b * BLOCK + TOK : b * BLOCK + BLOCK, :].astype(F32)
                    parts = [packed[:, ROPE * c : ROPE * c + ROPE] for c in range(8)]
                    acc_r[i, b * TOK : b * TOK + TOK, :] = jnp.concatenate(parts, axis=0)
            else:
                acc[i] = jnp.zeros((512, LATENT), F32)
                acc_r[i] = jnp.zeros((512, ROPE), F32)

    for k in range(2):

        @pl.when(kk == k)
        def _():
            w[...] = given[k][...]

    weights = w[...]
    w_t[...] = weights.T
    for j in range(4):
        kv = dot(lat[j], weights).astype(BF)
        for h in range(2):
            kn[h, j] = kv[:, h * 128 : h * 128 + 128]
            vs[h, j] = kv[:, 256 + h * 128 : 384 + h * 128]
    rows = pl.ds(pl.multiple_of(kk * TOK, TOK), TOK)
    for i in range(4):
        lane = lax.broadcasted_iota(jnp.int32, (TOK, ROPE), 1)
        ones = jnp.where((lane == 0) | (lane == 1 + i), 1.0, 0.0).astype(BF)
        for h in range(2):
            qs[h, i] = jnp.concatenate([msgs[i, rows, h * QK : h * QK + QK], ones], axis=1)
            gs[h, i] = msgs[i, rows, PAIR + h * VDIM : PAIR + (h + 1) * VDIM]
            lanes = pl.ds(pl.multiple_of((2 * kk + h) * TOK, TOK), TOK)
            part = jnp.sum(msgs[i, 2 * TOK :, lanes].astype(F32), axis=0, keepdims=True)
            dl[h, i] = jnp.broadcast_to(part, (8, TOK))

    r = lax.broadcasted_iota(jnp.int32, (128, 128), 0)
    c = lax.broadcasted_iota(jnp.int32, (128, 128), 1)
    for h in range(2):
        q = qs[h].reshape(512, 256)
        q_t = q.T
        peaks = [None] * 4
        for j in range(4):
            keys = jnp.concatenate([kn[h, j], kx[j]], axis=1)
            sj = dot(keys, q_t[:, 128 * j :])
            pos = 512 * j + 128 * z + r
            own = jnp.where(r <= c, sj[:128, :128], BIG)
            own = jnp.where((r == c) & (pos < off), 0.0, own)
            slabs[j][:128, :128] = own
            if j < 3:
                slabs[j][:128, 128:] = sj[:128, 128:]
            slabs[j][128:, :] = sj[128:, :]
            top = jnp.max(sj[128:, :], axis=0, keepdims=True)
            head = jnp.max(own, axis=0, keepdims=True)
            if j < 3:
                head = jnp.concatenate([head, jnp.max(sj[:128, 128:], axis=0, keepdims=True)], axis=1)
            top = jnp.maximum(top, head)
            for i in range(j, 4):
                piece = top[:, 128 * (i - j) : 128 * (i - j) + 128]
                peaks[i] = piece if peaks[i] is None else jnp.maximum(peaks[i], piece)
        peak = jnp.concatenate(peaks, axis=1)
        total = jnp.zeros((1, 512), F32)
        for j in range(4):
            e = jnp.exp2((slabs[j][...] - peak[:, 128 * j :]) * (SCALE * LOG2E))
            slabs[j][...] = e
            add = jnp.sum(e, axis=0, keepdims=True)
            if j:
                add = jnp.concatenate([jnp.zeros((1, 128 * j), F32), add], axis=1)
            total = total + add
        inv = 1.0 / total
        g_t = gs[h].reshape(512, VDIM).T
        gn_t = (g_t.astype(F32) * inv).astype(BF)
        gn = gn_t.T
        delta = jnp.concatenate([dl[h, i][:1] for i in range(4)], axis=1) * inv
        dq_t = jnp.zeros((QK, 512), F32)
        for j in range(4):
            cut = slice(128 * j, 512)
            e = slabs[j][...]
            dp = dot(vs[h, j], gn_t[:, cut])
            ds = (e * (dp - delta[:, cut])).astype(BF)
            dv = dot(e.astype(BF), gn[cut])
            dk = dot(ds, q[cut]) * SCALE
            dkv[j, :, h * 128 : h * 128 + 128] = dk[:, :NOPE].astype(BF)
            dkv[j, :, 256 + h * 128 : 384 + h * 128] = dv.astype(BF)
            acc_r[j] += dk[:, NOPE:QK]
            keys_t = jnp.concatenate([kn[h, j].T, kx_t[j][:ROPE]], axis=0)
            add = dot(keys_t, ds)
            if j:
                add = jnp.concatenate([jnp.zeros((QK, 128 * j), F32), add], axis=1)
            dq_t = dq_t + add
        dq = (dq_t * SCALE).T.astype(BF)
        for i in range(4):
            dq_scr[i, :, h * QK : h * QK + QK] = dq[128 * i : 128 * i + 128]

    total_w = None
    for j in range(4):
        both = dkv[j]
        acc[j] += dot(both, w_t[...])
        add = dot(lat_t[j], both)
        total_w = add if total_w is None else total_w + add
    gw[...] = total_w
    for i in range(4):
        if has_prior:
            dqs[i][...] = dq_scr[(x + i) & 3]
        else:
            dqs[0][i] = dq_scr[i]
    for s in range(4):
        at = ((y + s) & 3) * 64
        gkeep[s, 0] = gw[pl.ds(pl.multiple_of(core * 256 + at, 64), 64), :].astype(BF)
        gsend[s, 0] = gw[pl.ds(pl.multiple_of((1 - core) * 256 + at, 64), 64), :].astype(BF)

    @pl.when(kk == 1)
    def _():
        for s in range(4):
            i = (x + s) & 3
            for b in range(4):
                gls[s][b * BLOCK : b * BLOCK + TOK, :] = acc[i, b * TOK : b * TOK + TOK, :].astype(BF)
                parts = [acc_r[i, b * TOK + 16 * c : b * TOK + 16 * c + 16, :] for c in range(8)]
                gls[s][b * BLOCK + TOK : b * BLOCK + BLOCK, :] = jnp.concatenate(parts, axis=1).astype(BF)


def attention(sc, msgs, lats, w_all, priors):
    def whole(shape):
        return pl.BlockSpec(shape, lambda k, sc: (0,) * len(shape))

    has_prior = priors is not None
    slab = whole((SLAB, LATENT))
    in_specs = [whole((4, 2 * TOK + 16, MSG))] + [slab] * 4 + [whole((512, 512))] * 2
    args = [msgs, *lats, *w_all]
    if has_prior:
        in_specs += [slab] * 4
        args += list(priors)
        out_specs = [pl.BlockSpec((TOK, PAIR), lambda k, sc: (k, 0))] * 4
        out_shape = [jax.ShapeDtypeStruct((2 * TOK, PAIR), BF)] * 4
    else:
        out_specs = [pl.BlockSpec((4, TOK, PAIR), lambda k, sc: (0, k, 0))]
        out_shape = [jax.ShapeDtypeStruct((4, 2 * TOK, PAIR), BF)]
    out_specs += [slab] * 4 + [pl.BlockSpec((4, 1, 64, 512), lambda k, sc: (0, k, 0, 0))] * 2
    out_shape += [jax.ShapeDtypeStruct((SLAB, LATENT), BF)] * 4 + [jax.ShapeDtypeStruct((4, 2, 64, 512), BF)] * 2
    scratch = [
        pltpu.VMEM((4, 512, LATENT), BF),
        pltpu.VMEM((4, LATENT, 512), BF),
        pltpu.VMEM((4, 512, 128), BF),
        pltpu.VMEM((4, 128, 512), BF),
        pltpu.VMEM((4, 512, LATENT), F32),
        pltpu.VMEM((4, 512, ROPE), F32),
        pltpu.VMEM((512, 512), BF),
        pltpu.VMEM((512, 512), BF),
        pltpu.VMEM((2, 4, 512, 128), BF),
        pltpu.VMEM((2, 4, 512, 128), BF),
        pltpu.VMEM((2, 4, TOK, 256), BF),
        pltpu.VMEM((2, 4, TOK, VDIM), BF),
        pltpu.VMEM((2, 4, 8, TOK), F32),
        pltpu.VMEM((4, 512, 512), BF),
        pltpu.VMEM((4, TOK, PAIR), BF),
        pltpu.VMEM((512, 512), F32),
        pltpu.VMEM((512, 512), F32),
        pltpu.VMEM((512, 384), F32),
        pltpu.VMEM((512, 256), F32),
        pltpu.VMEM((512, 128), F32),
    ]
    outs = pl.pallas_call(
        functools.partial(attn_kernel, has_prior),
        grid_spec=pltpu.PrefetchScalarGridSpec(
            num_scalar_prefetch=1, grid=(2,), in_specs=in_specs, out_specs=out_specs, scratch_shapes=scratch
        ),
        out_shape=out_shape,
        compiler_params=pltpu.CompilerParams(vmem_limit_bytes=56 * 1024 * 1024),
        cost_estimate=pl.CostEstimate(flops=25_000_000_000, bytes_accessed=10_000_000, transcendentals=2_700_000),
        name="attention",
    )(sc, *args)
    return outs[:-6], outs[-6:-2], outs[-2], outs[-1]


def unpack_kernel(sc, first, s0, s1, s2, s3, out):
    for kk in range(2):
        rows = slice(kk * TOK, kk * TOK + TOK)
        for i in range(4):
            group = (sc[0] + GROUPS[0][kk]) & 3
            out[:, pl.ds(pl.multiple_of((i * NZ + group) * PAIR, 128), PAIR)] = first[i, rows, :]
        for s, ref in enumerate((s0, s1, s2, s3)):
            group = (sc[0] + GROUPS[1][kk]) & 3
            lanes = pl.multiple_of((((sc[3] - s) & 3) * NZ + group) * PAIR, 128)
            out[:, pl.ds(lanes, PAIR)] = ref[rows, :]


def unpack(sc, first, second):
    spec = pl.BlockSpec(memory_space=pltpu.VMEM)
    return pl.pallas_call(
        unpack_kernel,
        in_specs=[pl.BlockSpec(memory_space=pltpu.SMEM)] + [spec] * 5,
        out_specs=spec,
        out_shape=jax.ShapeDtypeStruct((TOK, 16 * PAIR), BF),
        cost_estimate=pl.CostEstimate(flops=0, bytes_accessed=3_000_000, transcendentals=0),
        name="unpack",
    )(sc, first, *second)


def weights_kernel(sc, mine, other, out_k, out_v):
    core = sc[2]
    for base, ref in ((core, mine), (1 - core, other)):
        rows = pl.ds(pl.multiple_of(base * 256, 256), 256)
        for h in range(2):
            out_k[rows, h, :] = ref[:, h * 128 : h * 128 + 128].astype(F32)
            out_v[rows, h, :] = ref[:, 256 + h * 128 : 384 + h * 128].astype(F32)


def place_weights(sc, mine, other):
    spec = pl.BlockSpec(memory_space=pltpu.VMEM)
    return pl.pallas_call(
        weights_kernel,
        in_specs=[pl.BlockSpec(memory_space=pltpu.SMEM)] + [spec] * 2,
        out_specs=[spec] * 2,
        out_shape=[jax.ShapeDtypeStruct((512, 2, 128), F32)] * 2,
        cost_estimate=pl.CostEstimate(flops=0, bytes_accessed=2_000_000, transcendentals=0),
        name="place_weights",
    )(sc, mine, other)


def barrier(*values):
    return lax.optimization_barrier(values)


def summed(parts):
    total = parts[0].astype(F32)
    for n in range(1, len(parts)):
        total = total + parts[n].astype(F32)
    return total


def shards(query, latent, rope_key, grad_mantissa, grad_exponent, forward_out, offsets, w_key, w_value):
    dp, seq = lax.axis_index("dp"), lax.axis_index("seq")
    sc = jnp.stack([seq & 3, offsets[0], dp & 1, seq >> 2, dp >> 2]).astype(jnp.int32)

    ropes = rope_key[0].reshape(8, 16, ROPE).transpose(1, 0, 2).reshape(16, LATENT)
    own = jnp.concatenate([latent[0], ropes], axis=0)
    w_own = jnp.concatenate([w_key.reshape(LATENT, 256), w_value.reshape(LATENT, 256)], axis=1)
    near = [send(w_own, ring=-1), send(w_own, ring=1)]
    slab = jnp.concatenate([own] + [send(own, dz=s) for s in (1, 2, 3)], axis=0)

    inputs = (query[0], grad_mantissa[0], grad_exponent[0], forward_out[0])
    packed = pack(GROUPS[0], sc, *inputs)
    first = trade(packed, "x")
    slab, packed, *near = barrier(slab, packed, *near)
    lats = [slab] + [send(slab, dx=s) for s in (1, 2, 3)]

    first, w_held = barrier(first, w_own)
    far = jnp.concatenate([send(w_held[:256], ring=-2), send(w_held[256:], ring=2)], axis=0)
    *lats, far, packed = barrier(*lats, far, pack(GROUPS[1], sc, *inputs))
    second = trade(packed, "x")
    w_all = [w_own, near[0], far, near[1]]

    dqs, priors, keep, away = attention(sc, first, lats, [w_all[k] for k in GROUPS[0]], None)
    back = trade(dqs[0], "x")
    both = (keep.astype(F32) + send(away, dc=1).astype(F32)).astype(BF)
    dqs, priors, keep, away = attention(sc, second, lats, [w_all[k] for k in GROUPS[1]], priors)
    *priors, away, both, back = barrier(*priors, away, both, back)

    along_x = summed([priors[0]] + [send(priors[s], dx=s) for s in (1, 2, 3)]).astype(BF)
    along_x, *dqs = barrier(along_x, *dqs)
    blocks = along_x.reshape(NZ, BLOCK, LATENT)
    along_z = summed([blocks[0]] + [send(blocks[s], dz=-s) for s in (1, 2, 3)])
    grad_query = unpack(sc, back, [dqs[0]] + [send(dqs[s], dx=s) for s in (1, 2, 3)])

    both = jnp.concatenate([both, (keep.astype(F32) + send(away, dc=1).astype(F32)).astype(BF)], axis=1)
    partial = summed([both[0]] + [send(both[s], dy=s) for s in (1, 2, 3)]).astype(BF)
    by_group = {k: partial[n] for n, k in enumerate(GROUPS[0] + GROUPS[1])}
    own_heads = summed([by_group[0]] + [send(by_group[k], ring=(0, 1, 2, -1)[k]) for k in (1, 2, 3)]).astype(BF)
    own_heads = (own_heads.astype(F32) + send(own_heads, ring=4).astype(F32)).astype(BF)
    mine = spread(own_heads, "y").reshape(256, 512)
    total_key, total_value = place_weights(sc, mine, send(mine, dc=1))
    grad_rope = along_z[TOK:].reshape(16, 8, ROPE).transpose(1, 0, 2).reshape(TOK, ROPE)
    return grad_query[None], along_z[None, :TOK], grad_rope[None], total_key, total_value


def solution(mesh):
    tokens = P("dp", "seq", None)
    heads = P(None, "seq", None)
    in_specs = (tokens,) * 6 + (P("dp"), heads, heads)
    out_specs = (tokens,) * 3 + (heads, heads)
    return jax.shard_map(shards, mesh=mesh, in_specs=in_specs, out_specs=out_specs, check_vma=False)
```

```python
import functools

import jax
import jax.numpy as jnp
import numpy as np
from jax import lax
from jax.experimental import pallas as pl
from jax.experimental.pallas import tpu as pltpu
from jax.sharding import PartitionSpec as P

LATENT = 512
ROPE = 64
NOPE = 128
VDIM = 128
QK = NOPE + ROPE
TOK = 128
PAIR = 2 * QK
MSG = PAIR + 2 * VDIM
BLOCK = TOK + 16
SLAB = 4 * BLOCK
GROUPS = ((0, 1), (3, 2))
SCALE = QK ** (-0.5)
LOG2E = 1.4426950408889634
BIG = -1e30
NY, NZH, NC, NX, NZ = 4, 2, 2, 4, 4
BF, F32 = jnp.bfloat16, jnp.float32


def dot(a, b):
    return jnp.dot(a, b, preferred_element_type=F32)


def moves(dy=0, dc=0, dx=0, dz=0, ring=0):
    pairs = []
    shape = (NY, NZH, NC, NX, NZ)
    for index in np.ndindex(*shape):
        y, zh, c, x, z = index
        along = (zh * NZ + z + ring) % (NZH * NZ)
        dest = ((y + dy) % NY, along // NZ, (c + dc) % NC, (x + dx) % NX, (along + dz) % NZ)
        pairs.append((int(np.ravel_multi_index(index, shape)), int(np.ravel_multi_index(dest, shape))))
    return pairs


def send(value, **shift):
    return lax.ppermute(value, ("dp", "seq"), moves(**shift))


def trade(value, axis):
    groups = {
        "x": [[z + NZ * x for x in range(NX)] for z in range(NZ)],
        "z": [[z + NZ * x for z in range(NZ)] for x in range(NX)],
        "y": [[r + NZH * NC * y for y in range(NY)] for r in range(NZH * NC)],
    }[axis]
    return lax.all_to_all(value, "dp" if axis == "y" else "seq", 0, 0, axis_index_groups=groups)


def spread(value, axis):
    return trade(jnp.broadcast_to(value[None], (4, *value.shape)), axis)


def pack_kernel(groups, sc, q0, q1, m0, m1, f0, f1, ex, out):
    step = pl.program_id(0)
    for kk, (q, m, f) in enumerate(((q0, m0, f0), (q1, m1, f1))):
        rows = slice(kk * TOK, kk * TOK + TOK)
        exps = ex[...].T
        lane = lax.broadcasted_iota(jnp.int32, exps.shape, 1)
        grads, deltas = [], []
        for h in range(2):
            e = jnp.sum(jnp.where(lane == 2 * (step * NZ + ((sc[0] + groups[kk]) & 3)) + h, exps, 0), axis=1, keepdims=True)
            scale = jnp.left_shift(jnp.ones_like(e), e + 3).astype(F32) * 0.125
            part = slice(h * VDIM, (h + 1) * VDIM)
            g = (m[:, part].astype(F32) * scale).astype(BF)
            grads.append(g)
            prod = g.astype(F32) * f[:, part].astype(F32)
            d = jnp.sum(prod.T, axis=0, keepdims=True)
            hi = d.astype(BF).astype(F32)
            mid = (d - hi).astype(BF).astype(F32)
            row = lax.broadcasted_iota(jnp.int32, (16, TOK), 0)
            deltas.append(
                jnp.where(row == 0, hi, jnp.where(row == 1, mid, jnp.where(row == 2, d - hi - mid, 0.0)))
            )
        out[0, rows, :PAIR] = q[...]
        out[0, rows, PAIR : PAIR + VDIM] = grads[0]
        out[0, rows, PAIR + VDIM :] = grads[1]
        out[0, 2 * TOK :, kk * 256 : kk * 256 + 256] = jnp.concatenate(deltas, axis=1).astype(BF)
    out[0, 2 * TOK :, 512:] = jnp.zeros((16, MSG - 512), BF)


def pack(groups, sc, query, mantissa, exponent, saved):
    def at(kk):
        return lambda s, sc: (0, s * NZ + ((sc[0] + groups[kk]) & 3))

    return pl.pallas_call(
        functools.partial(pack_kernel, groups),
        grid_spec=pltpu.PrefetchScalarGridSpec(
            num_scalar_prefetch=1,
            grid=(4,),
            in_specs=[
                pl.BlockSpec((TOK, PAIR), at(0)),
                pl.BlockSpec((TOK, PAIR), at(1)),
                pl.BlockSpec((TOK, 256), at(0)),
                pl.BlockSpec((TOK, 256), at(1)),
                pl.BlockSpec((TOK, 256), at(0)),
                pl.BlockSpec((TOK, 256), at(1)),
                pl.BlockSpec((32, TOK), lambda s, sc: (0, 0)),
            ],
            out_specs=pl.BlockSpec((1, 2 * TOK + 16, MSG), lambda s, sc: (s, 0, 0)),
        ),
        out_shape=jax.ShapeDtypeStruct((4, 2 * TOK + 16, MSG), BF),
        cost_estimate=pl.CostEstimate(flops=2_000_000, bytes_accessed=4_000_000, transcendentals=0),
        name="pack",
    )(sc, query, query, mantissa, mantissa, saved, saved, exponent)


def attn_kernel(sc, *refs):
    msgs, lats, given = refs[0:2], refs[2:6], refs[6:10]
    dqs, gls, gkeep, gsend = refs[10:14], refs[14:18], refs[18], refs[19]
    lat, lat_t, kx, kx_t, acc, acc_r, w, w_t, kn, vs, qs, gs, dl, dkv, dq_scr, gw, s0, s1, s2, s3 = refs[20:]
    slabs = (s0, s1, s2, s3)
    kk = pl.program_id(0)
    z, off, core, x, y = sc[0], sc[1], sc[2], sc[3], sc[4]

    @pl.when(kk == 0)
    def _():
        for s in range(4):
            j = (x - s) & 3
            ropes = []
            for b in range(4):
                block = lats[s][b * BLOCK : b * BLOCK + TOK, :]
                lat[j, b * TOK : b * TOK + TOK, :] = block
                lat_t[j, :, b * TOK : b * TOK + TOK] = block.T
                packed = lats[s][b * BLOCK + TOK : b * BLOCK + BLOCK, :]
                ropes += [packed[:, ROPE * c : ROPE * c + ROPE] for c in range(8)]
            r = lax.broadcasted_iota(jnp.int32, (512, ROPE), 0)
            lane = lax.broadcasted_iota(jnp.int32, (512, ROPE), 1)
            blk = r >> 7
            pos = 512 * j + 128 * ((z - blk) & 3) + (r & 127)
            hide = ((lane == 0) & (pos < off)) | ((lane == 1 + j) & (blk > z))
            extra = jnp.where(hide, BIG, 0.0).astype(BF)
            both = jnp.concatenate([jnp.concatenate(ropes, axis=0), extra], axis=1)
            kx[j] = both
            kx_t[j] = both.T
            acc[j] = jnp.zeros((512, LATENT), F32)
            acc_r[j] = jnp.zeros((512, ROPE), F32)

    for k in range(4):

        @pl.when(kk == k)
        def _():
            w[...] = given[k][...]

    weights = w[...]
    w_t[...] = weights.T
    for j in range(4):
        kv = dot(lat[j], weights).astype(BF)
        for h in range(2):
            kn[h, j] = kv[:, h * 128 : h * 128 + 128]
            vs[h, j] = kv[:, 256 + h * 128 : 384 + h * 128]
    for n in range(2):

        @pl.when((kk >> 1) == n)
        def _():
            rows = pl.ds(pl.multiple_of((kk & 1) * TOK, TOK), TOK)
            for i in range(4):
                lane = lax.broadcasted_iota(jnp.int32, (TOK, ROPE), 1)
                ones = jnp.where((lane == 0) | (lane == 1 + i), 1.0, 0.0).astype(BF)
                for h in range(2):
                    qs[h, i] = jnp.concatenate([msgs[n][i, rows, h * QK : h * QK + QK], ones], axis=1)
                    gs[h, i] = msgs[n][i, rows, PAIR + h * VDIM : PAIR + (h + 1) * VDIM]
                    lanes = pl.ds(pl.multiple_of((2 * (kk & 1) + h) * TOK, TOK), TOK)
                    part = jnp.sum(msgs[n][i, 2 * TOK :, lanes].astype(F32), axis=0, keepdims=True)
                    dl[h, i] = jnp.broadcast_to(part, (8, TOK))

    r = lax.broadcasted_iota(jnp.int32, (128, 128), 0)
    c = lax.broadcasted_iota(jnp.int32, (128, 128), 1)
    for h in range(2):
        q = qs[h].reshape(512, 256)
        q_t = q.T
        peaks = [None] * 4
        for j in range(4):
            keys = jnp.concatenate([kn[h, j], kx[j]], axis=1)
            sj = dot(keys, q_t[:, 128 * j :])
            pos = 512 * j + 128 * z + r
            own = jnp.where(r <= c, sj[:128, :128], BIG)
            own = jnp.where((r == c) & (pos < off), 0.0, own)
            slabs[j][:128, :128] = own
            if j < 3:
                slabs[j][:128, 128:] = sj[:128, 128:]
            slabs[j][128:, :] = sj[128:, :]
            top = jnp.max(sj[128:, :], axis=0, keepdims=True)
            head = jnp.max(own, axis=0, keepdims=True)
            if j < 3:
                head = jnp.concatenate([head, jnp.max(sj[:128, 128:], axis=0, keepdims=True)], axis=1)
            top = jnp.maximum(top, head)
            for i in range(j, 4):
                piece = top[:, 128 * (i - j) : 128 * (i - j) + 128]
                peaks[i] = piece if peaks[i] is None else jnp.maximum(peaks[i], piece)
        peak = jnp.concatenate(peaks, axis=1)
        total = jnp.zeros((1, 512), F32)
        for j in range(4):
            e = jnp.exp2((slabs[j][...] - peak[:, 128 * j :]) * (SCALE * LOG2E))
            slabs[j][...] = e
            add = jnp.sum(e, axis=0, keepdims=True)
            if j:
                add = jnp.concatenate([jnp.zeros((1, 128 * j), F32), add], axis=1)
            total = total + add
        inv = 1.0 / total
        g_t = gs[h].reshape(512, VDIM).T
        gn_t = (g_t.astype(F32) * inv).astype(BF)
        gn = gn_t.T
        delta = jnp.concatenate([dl[h, i][:1] for i in range(4)], axis=1) * inv
        dq_t = jnp.zeros((QK, 512), F32)
        for j in range(4):
            cut = slice(128 * j, 512)
            e = slabs[j][...]
            dp = dot(vs[h, j], gn_t[:, cut])
            ds = (e * (dp - delta[:, cut])).astype(BF)
            dv = dot(e.astype(BF), gn[cut])
            dk = dot(ds, q[cut]) * SCALE
            dkv[j, :, h * 128 : h * 128 + 128] = dk[:, :NOPE].astype(BF)
            dkv[j, :, 256 + h * 128 : 384 + h * 128] = dv.astype(BF)
            acc_r[j] += dk[:, NOPE:QK]
            keys_t = jnp.concatenate([kn[h, j].T, kx_t[j][:ROPE]], axis=0)
            add = dot(keys_t, ds)
            if j:
                add = jnp.concatenate([jnp.zeros((QK, 128 * j), F32), add], axis=1)
            dq_t = dq_t + add
        dq = (dq_t * SCALE).T.astype(BF)
        for i in range(4):
            dq_scr[i, :, h * QK : h * QK + QK] = dq[128 * i : 128 * i + 128]

    total_w = None
    for j in range(4):
        both = dkv[j]
        acc[j] += dot(both, w_t[...])
        add = dot(lat_t[j], both)
        total_w = add if total_w is None else total_w + add
    gw[...] = total_w
    for i in range(4):
        dqs[i][...] = dq_scr[(x + i) & 3]
    for s in range(4):
        at = ((y + s) & 3) * 64
        gkeep[s, 0] = gw[pl.ds(pl.multiple_of(core * 256 + at, 64), 64), :].astype(BF)
        gsend[s, 0] = gw[pl.ds(pl.multiple_of((1 - core) * 256 + at, 64), 64), :].astype(BF)

    @pl.when(kk == 3)
    def _():
        for s in range(4):
            i = (x + s) & 3
            for b in range(4):
                gls[s][b * BLOCK : b * BLOCK + TOK, :] = acc[i, b * TOK : b * TOK + TOK, :].astype(BF)
                parts = [acc_r[i, b * TOK + 16 * c : b * TOK + 16 * c + 16, :] for c in range(8)]
                gls[s][b * BLOCK + TOK : b * BLOCK + BLOCK, :] = jnp.concatenate(parts, axis=1).astype(BF)


def attention(sc, msgs, lats, w_all):
    def whole(shape):
        return pl.BlockSpec(shape, lambda k, sc: (0,) * len(shape))

    slab = whole((SLAB, LATENT))
    in_specs = [whole((4, 2 * TOK + 16, MSG))] * 2 + [slab] * 4 + [whole((512, 512))] * 4
    args = [*msgs, *lats, *w_all]
    out_specs = [pl.BlockSpec((TOK, PAIR), lambda k, sc: (k, 0))] * 4
    out_shape = [jax.ShapeDtypeStruct((4 * TOK, PAIR), BF)] * 4
    out_specs += [slab] * 4 + [pl.BlockSpec((4, 1, 64, 512), lambda k, sc: (0, k, 0, 0))] * 2
    out_shape += [jax.ShapeDtypeStruct((SLAB, LATENT), BF)] * 4 + [jax.ShapeDtypeStruct((4, 4, 64, 512), BF)] * 2
    scratch = [
        pltpu.VMEM((4, 512, LATENT), BF),
        pltpu.VMEM((4, LATENT, 512), BF),
        pltpu.VMEM((4, 512, 128), BF),
        pltpu.VMEM((4, 128, 512), BF),
        pltpu.VMEM((4, 512, LATENT), F32),
        pltpu.VMEM((4, 512, ROPE), F32),
        pltpu.VMEM((512, 512), BF),
        pltpu.VMEM((512, 512), BF),
        pltpu.VMEM((2, 4, 512, 128), BF),
        pltpu.VMEM((2, 4, 512, 128), BF),
        pltpu.VMEM((2, 4, TOK, 256), BF),
        pltpu.VMEM((2, 4, TOK, VDIM), BF),
        pltpu.VMEM((2, 4, 8, TOK), F32),
        pltpu.VMEM((4, 512, 512), BF),
        pltpu.VMEM((4, TOK, PAIR), BF),
        pltpu.VMEM((512, 512), F32),
        pltpu.VMEM((512, 512), F32),
        pltpu.VMEM((512, 384), F32),
        pltpu.VMEM((512, 256), F32),
        pltpu.VMEM((512, 128), F32),
    ]
    outs = pl.pallas_call(
        attn_kernel,
        grid_spec=pltpu.PrefetchScalarGridSpec(
            num_scalar_prefetch=1, grid=(4,), in_specs=in_specs, out_specs=out_specs, scratch_shapes=scratch
        ),
        out_shape=out_shape,
        compiler_params=pltpu.CompilerParams(vmem_limit_bytes=56 * 1024 * 1024),
        cost_estimate=pl.CostEstimate(flops=50_000_000_000, bytes_accessed=14_000_000, transcendentals=5_400_000),
        name="attention",
    )(sc, *args)
    return outs[0:4], outs[4:8], outs[8], outs[9]


def unpack_kernel(sc, s0, s1, s2, s3, out):
    for kk, group in enumerate(GROUPS[0] + GROUPS[1]):
        for s, ref in enumerate((s0, s1, s2, s3)):
            lanes = pl.multiple_of((((sc[3] - s) & 3) * NZ + ((sc[0] + group) & 3)) * PAIR, 128)
            out[:, pl.ds(lanes, PAIR)] = ref[kk * TOK : kk * TOK + TOK, :]


def unpack(sc, pieces):
    spec = pl.BlockSpec(memory_space=pltpu.VMEM)
    return pl.pallas_call(
        unpack_kernel,
        in_specs=[pl.BlockSpec(memory_space=pltpu.SMEM)] + [spec] * 4,
        out_specs=spec,
        out_shape=jax.ShapeDtypeStruct((TOK, 16 * PAIR), BF),
        cost_estimate=pl.CostEstimate(flops=0, bytes_accessed=3_000_000, transcendentals=0),
        name="unpack",
    )(sc, *pieces)


def latents_kernel(b0, b1, b2, b3, out, out_rope):
    total = summed([b[...] for b in (b0, b1, b2, b3)])
    out[...] = total[:TOK]
    out_rope[...] = jnp.concatenate([total[TOK:, ROPE * c : ROPE * c + ROPE] for c in range(8)], axis=0).T


def finish_latents(pieces):
    spec = pl.BlockSpec(memory_space=pltpu.VMEM)
    return pl.pallas_call(
        latents_kernel,
        in_specs=[spec] * 4,
        out_specs=[spec] * 2,
        out_shape=[jax.ShapeDtypeStruct((TOK, LATENT), F32), jax.ShapeDtypeStruct((ROPE, TOK), F32)],
        cost_estimate=pl.CostEstimate(flops=20_000_000_000, bytes_accessed=1_000_000, transcendentals=0),
        name="finish_latents",
    )(*pieces)


def weights_kernel(sc, mine, other, out_k, out_v):
    core = sc[2]
    for base, ref in ((core, mine), (1 - core, other)):
        rows = pl.ds(pl.multiple_of(base * 256, 256), 256)
        for h in range(2):
            out_k[rows, h, :] = ref[:, h * 128 : h * 128 + 128].astype(F32)
            out_v[rows, h, :] = ref[:, 256 + h * 128 : 384 + h * 128].astype(F32)


def place_weights(sc, mine, other):
    spec = pl.BlockSpec(memory_space=pltpu.VMEM)
    return pl.pallas_call(
        weights_kernel,
        in_specs=[pl.BlockSpec(memory_space=pltpu.SMEM)] + [spec] * 2,
        out_specs=[spec] * 2,
        out_shape=[jax.ShapeDtypeStruct((512, 2, 128), F32)] * 2,
        cost_estimate=pl.CostEstimate(flops=0, bytes_accessed=2_000_000, transcendentals=0),
        name="place_weights",
    )(sc, mine, other)


def barrier(*values):
    return lax.optimization_barrier(values)


def summed(parts):
    total = parts[0].astype(F32)
    for n in range(1, len(parts)):
        total = total + parts[n].astype(F32)
    return total


def shards(query, latent, rope_key, grad_mantissa, grad_exponent, forward_out, offsets, w_key, w_value):
    dp, seq = lax.axis_index("dp"), lax.axis_index("seq")
    sc = jnp.stack([seq & 3, offsets[0], dp & 1, seq >> 2, dp >> 2]).astype(jnp.int32)

    ropes = rope_key[0].reshape(8, 16, ROPE).transpose(1, 0, 2).reshape(16, LATENT)
    own = jnp.concatenate([latent[0], ropes], axis=0)
    w_own = jnp.concatenate([w_key.reshape(LATENT, 256), w_value.reshape(LATENT, 256)], axis=1)
    near = [send(w_own, ring=-1), send(w_own, ring=1)]
    slab = jnp.concatenate([own] + [send(own, dz=s) for s in (1, 2, 3)], axis=0)

    inputs = (query[0], grad_mantissa[0], grad_exponent[0].T, forward_out[0])
    packed = pack(GROUPS[0], sc, *inputs)
    first = trade(packed, "x")
    slab, packed, *near = barrier(slab, packed, *near)
    lats = [slab] + [send(slab, dx=s) for s in (1, 2, 3)]

    first, w_held, packed = barrier(first, w_own, pack(GROUPS[1], sc, *inputs))
    far = jnp.concatenate([send(w_held[:256], ring=-2), send(w_held[256:], ring=2)], axis=0)
    second = trade(packed, "x")
    w_all = [w_own, near[0], far, near[1]]

    w_all = [w_all[k] for k in GROUPS[0] + GROUPS[1]]
    dqs, priors, keep, away = attention(sc, (first, second), lats, w_all)

    along_x = summed([priors[0]] + [send(priors[s], dx=s) for s in (1, 2, 3)]).astype(BF)
    blocks = along_x.reshape(NZ, BLOCK, LATENT)
    grad_latent, grad_rope = finish_latents([blocks[0]] + [send(blocks[s], dz=-s) for s in (1, 2, 3)])

    both = (keep.astype(F32) + send(away, dc=1).astype(F32)).astype(BF)
    partial = summed([both[0]] + [send(both[s], dy=s) for s in (1, 2, 3)]).astype(BF)
    by_group = {k: partial[n] for n, k in enumerate(GROUPS[0] + GROUPS[1])}
    own_heads = summed([by_group[0]] + [send(by_group[k], ring=(0, 1, 2, -1)[k]) for k in (1, 2, 3)]).astype(BF)
    grad_query = unpack(sc, [dqs[0]] + [send(dqs[s], dx=s) for s in (1, 2, 3)])
    own_heads = (own_heads.astype(F32) + send(own_heads, ring=4).astype(F32)).astype(BF)
    mine = spread(own_heads, "y").reshape(256, 512)
    total_key, total_value = place_weights(sc, mine, send(mine, dc=1))
    return grad_query[None], grad_latent[None], grad_rope.T[None], total_key, total_value


def solution(mesh):
    tokens = P("dp", "seq", None)
    heads = P(None, "seq", None)
    in_specs = (tokens,) * 6 + (P("dp"), heads, heads)
    out_specs = (tokens,) * 3 + (heads, heads)
    return jax.shard_map(shards, mesh=mesh, in_specs=in_specs, out_specs=out_specs, check_vma=False)
```

```python
import functools

import jax
import jax.numpy as jnp
import numpy as np
from jax import lax
from jax.experimental import pallas as pl
from jax.experimental.pallas import tpu as pltpu
from jax.sharding import PartitionSpec as P

LATENT = 512
ROPE = 64
NOPE = 128
VDIM = 128
QK = NOPE + ROPE
TOK = 128
PAIR = 2 * QK
MSG = PAIR + 2 * VDIM
BLOCK = TOK + 16
SLAB = 4 * BLOCK
GROUPS = ((0, 1), (3, 2))
SCALE = QK ** (-0.5)
LOG2E = 1.4426950408889634
BIG = -1e30
NY, NZH, NC, NX, NZ = 4, 2, 2, 4, 4
BF, F32 = jnp.bfloat16, jnp.float32


def dot(a, b):
    return jnp.dot(a, b, preferred_element_type=F32)


def moves(dy=0, dc=0, dx=0, dz=0, ring=0):
    pairs = []
    shape = (NY, NZH, NC, NX, NZ)
    for index in np.ndindex(*shape):
        y, zh, c, x, z = index
        along = (zh * NZ + z + ring) % (NZH * NZ)
        dest = ((y + dy) % NY, along // NZ, (c + dc) % NC, (x + dx) % NX, (along + dz) % NZ)
        pairs.append((int(np.ravel_multi_index(index, shape)), int(np.ravel_multi_index(dest, shape))))
    return pairs


def send(value, **shift):
    return lax.ppermute(value, ("dp", "seq"), moves(**shift))


def trade(value, axis):
    groups = {
        "x": [[z + NZ * x for x in range(NX)] for z in range(NZ)],
        "z": [[z + NZ * x for z in range(NZ)] for x in range(NX)],
        "y": [[r + NZH * NC * y for y in range(NY)] for r in range(NZH * NC)],
    }[axis]
    return lax.all_to_all(value, "dp" if axis == "y" else "seq", 0, 0, axis_index_groups=groups)


def spread(value, axis):
    return trade(jnp.broadcast_to(value[None], (4, *value.shape)), axis)


def pack_kernel(groups, sc, q0, q1, m0, m1, f0, f1, ex, out):
    step = pl.program_id(0)
    for kk, (q, m, f) in enumerate(((q0, m0, f0), (q1, m1, f1))):
        rows = slice(kk * TOK, kk * TOK + TOK)
        exps = ex[...].T
        lane = lax.broadcasted_iota(jnp.int32, exps.shape, 1)
        grads, deltas = [], []
        for h in range(2):
            e = jnp.sum(jnp.where(lane == 2 * (step * NZ + ((sc[0] + groups[kk]) & 3)) + h, exps, 0), axis=1, keepdims=True)
            scale = jnp.left_shift(jnp.ones_like(e), e + 3).astype(F32) * 0.125
            part = slice(h * VDIM, (h + 1) * VDIM)
            g = (m[:, part].astype(F32) * scale).astype(BF)
            grads.append(g)
            prod = g.astype(F32) * f[:, part].astype(F32)
            d = jnp.sum(prod.T, axis=0, keepdims=True)
            hi = d.astype(BF).astype(F32)
            mid = (d - hi).astype(BF).astype(F32)
            row = lax.broadcasted_iota(jnp.int32, (16, TOK), 0)
            deltas.append(
                jnp.where(row == 0, hi, jnp.where(row == 1, mid, jnp.where(row == 2, d - hi - mid, 0.0)))
            )
        out[0, rows, :PAIR] = q[...]
        out[0, rows, PAIR : PAIR + VDIM] = grads[0]
        out[0, rows, PAIR + VDIM :] = grads[1]
        out[0, 2 * TOK :, kk * 256 : kk * 256 + 256] = jnp.concatenate(deltas, axis=1).astype(BF)
    out[0, 2 * TOK :, 512:] = jnp.zeros((16, MSG - 512), BF)


def pack(groups, sc, query, mantissa, exponent, saved):
    def at(kk):
        return lambda s, sc: (0, s * NZ + ((sc[0] + groups[kk]) & 3))

    return pl.pallas_call(
        functools.partial(pack_kernel, groups),
        grid_spec=pltpu.PrefetchScalarGridSpec(
            num_scalar_prefetch=1,
            grid=(4,),
            in_specs=[
                pl.BlockSpec((TOK, PAIR), at(0)),
                pl.BlockSpec((TOK, PAIR), at(1)),
                pl.BlockSpec((TOK, 256), at(0)),
                pl.BlockSpec((TOK, 256), at(1)),
                pl.BlockSpec((TOK, 256), at(0)),
                pl.BlockSpec((TOK, 256), at(1)),
                pl.BlockSpec((32, TOK), lambda s, sc: (0, 0)),
            ],
            out_specs=pl.BlockSpec((1, 2 * TOK + 16, MSG), lambda s, sc: (s, 0, 0)),
        ),
        out_shape=jax.ShapeDtypeStruct((4, 2 * TOK + 16, MSG), BF),
        cost_estimate=pl.CostEstimate(flops=2_000_000, bytes_accessed=4_000_000, transcendentals=0),
        name="pack",
    )(sc, query, query, mantissa, mantissa, saved, saved, exponent)


def attn_kernel(sc, *refs):
    msgs, lats, given = refs[0:2], refs[2:6], refs[6:10]
    dqs, gls, gkeep, gsend = refs[10:14], refs[14:18], refs[18], refs[19]
    lat, lat_t, kx, kx_t, acc, acc_r, w, w_t, kn, vs, qs, gs, dl, dkv, dq_scr, gw, s0, s1, s2, s3 = refs[20:]
    slabs = (s0, s1, s2, s3)
    kk = pl.program_id(0)
    z, off, core, x, y = sc[0], sc[1], sc[2], sc[3], sc[4]

    @pl.when(kk == 0)
    def _():
        for s in range(4):
            j = (x - s) & 3
            ropes = []
            for b in range(4):
                block = lats[s][b * BLOCK : b * BLOCK + TOK, :]
                lat[j, b * TOK : b * TOK + TOK, :] = block
                lat_t[j, :, b * TOK : b * TOK + TOK] = block.T
                packed = lats[s][b * BLOCK + TOK : b * BLOCK + BLOCK, :]
                ropes += [packed[:, ROPE * c : ROPE * c + ROPE] for c in range(8)]
            r = lax.broadcasted_iota(jnp.int32, (512, ROPE), 0)
            lane = lax.broadcasted_iota(jnp.int32, (512, ROPE), 1)
            blk = r >> 7
            pos = 512 * j + 128 * ((z - blk) & 3) + (r & 127)
            hide = ((lane == 0) & (pos < off)) | ((lane == 1 + j) & (blk > z))
            extra = jnp.where(hide, BIG, 0.0).astype(BF)
            both = jnp.concatenate([jnp.concatenate(ropes, axis=0), extra], axis=1)
            kx[j] = both
            kx_t[j] = both.T
            acc[j] = jnp.zeros((512, LATENT), F32)
            acc_r[j] = jnp.zeros((512, ROPE), F32)

    for k in range(4):

        @pl.when(kk == k)
        def _():
            w[...] = given[k][...]

    weights = w[...]
    w_t[...] = weights.T
    for j in range(4):
        kv = dot(lat[j], weights).astype(BF)
        for h in range(2):
            kn[h, j] = kv[:, h * 128 : h * 128 + 128]
            vs[h, j] = kv[:, 256 + h * 128 : 384 + h * 128]
    for n in range(2):

        @pl.when((kk >> 1) == n)
        def _():
            rows = pl.ds(pl.multiple_of((kk & 1) * TOK, TOK), TOK)
            for i in range(4):
                lane = lax.broadcasted_iota(jnp.int32, (TOK, ROPE), 1)
                ones = jnp.where((lane == 0) | (lane == 1 + i), 1.0, 0.0).astype(BF)
                for h in range(2):
                    qs[h, i] = jnp.concatenate([msgs[n][i, rows, h * QK : h * QK + QK], ones], axis=1)
                    gs[h, i] = msgs[n][i, rows, PAIR + h * VDIM : PAIR + (h + 1) * VDIM]
                    lanes = pl.ds(pl.multiple_of((2 * (kk & 1) + h) * TOK, TOK), TOK)
                    part = jnp.sum(msgs[n][i, 2 * TOK :, lanes].astype(F32), axis=0, keepdims=True)
                    dl[h, i] = jnp.broadcast_to(part, (8, TOK))

    r = lax.broadcasted_iota(jnp.int32, (128, 128), 0)
    c = lax.broadcasted_iota(jnp.int32, (128, 128), 1)
    for h in range(2):
        q = qs[h].reshape(512, 256)
        q_t = q.T
        peaks = [None] * 4
        for j in range(4):
            keys = jnp.concatenate([kn[h, j], kx[j]], axis=1)
            sj = dot(keys, q_t[:, 128 * j :])
            pos = 512 * j + 128 * z + r
            own = jnp.where(r <= c, sj[:128, :128], BIG)
            own = jnp.where((r == c) & (pos < off), 0.0, own)
            slabs[j][:128, :128] = own
            if j < 3:
                slabs[j][:128, 128:] = sj[:128, 128:]
            slabs[j][128:, :] = sj[128:, :]
            top = jnp.max(sj[128:, :], axis=0, keepdims=True)
            head = jnp.max(own, axis=0, keepdims=True)
            if j < 3:
                head = jnp.concatenate([head, jnp.max(sj[:128, 128:], axis=0, keepdims=True)], axis=1)
            top = jnp.maximum(top, head)
            for i in range(j, 4):
                piece = top[:, 128 * (i - j) : 128 * (i - j) + 128]
                peaks[i] = piece if peaks[i] is None else jnp.maximum(peaks[i], piece)
        peak = jnp.concatenate(peaks, axis=1)
        total = jnp.zeros((1, 512), F32)
        for j in range(4):
            e = jnp.exp2((slabs[j][...] - peak[:, 128 * j :]) * (SCALE * LOG2E))
            slabs[j][...] = e
            add = jnp.sum(e, axis=0, keepdims=True)
            if j:
                add = jnp.concatenate([jnp.zeros((1, 128 * j), F32), add], axis=1)
            total = total + add
        inv = 1.0 / total
        g_t = gs[h].reshape(512, VDIM).T
        gn_t = (g_t.astype(F32) * inv).astype(BF)
        gn = gn_t.T
        delta = jnp.concatenate([dl[h, i][:1] for i in range(4)], axis=1) * inv
        dq_t = jnp.zeros((QK, 512), F32)
        for j in range(4):
            cut = slice(128 * j, 512)
            e = slabs[j][...]
            dp = dot(vs[h, j], gn_t[:, cut])
            ds = (e * (dp - delta[:, cut])).astype(BF)
            dv = dot(e.astype(BF), gn[cut])
            dk = dot(ds, q[cut]) * SCALE
            dkv[j, :, h * 128 : h * 128 + 128] = dk[:, :NOPE].astype(BF)
            dkv[j, :, 256 + h * 128 : 384 + h * 128] = dv.astype(BF)
            acc_r[j] += dk[:, NOPE:QK]
            keys_t = jnp.concatenate([kn[h, j].T, kx_t[j][:ROPE]], axis=0)
            add = dot(keys_t, ds)
            if j:
                add = jnp.concatenate([jnp.zeros((QK, 128 * j), F32), add], axis=1)
            dq_t = dq_t + add
        dq = (dq_t * SCALE).T.astype(BF)
        for i in range(4):
            dq_scr[i, :, h * QK : h * QK + QK] = dq[128 * i : 128 * i + 128]

    total_w = None
    for j in range(4):
        both = dkv[j]
        acc[j] += dot(both, w_t[...])
        add = dot(lat_t[j], both)
        total_w = add if total_w is None else total_w + add
    gw[...] = total_w
    for i in range(4):
        dqs[i][...] = dq_scr[(x + i) & 3]
    for s in range(4):
        at = ((y + s) & 3) * 64
        gkeep[s, 0] = gw[pl.ds(pl.multiple_of(core * 256 + at, 64), 64), :].astype(BF)
        gsend[s, 0] = gw[pl.ds(pl.multiple_of((1 - core) * 256 + at, 64), 64), :].astype(BF)

    @pl.when(kk == 3)
    def _():
        for s in range(4):
            i = (x + s) & 3
            for b in range(4):
                gls[s][b * BLOCK : b * BLOCK + TOK, :] = acc[i, b * TOK : b * TOK + TOK, :].astype(BF)
                parts = [acc_r[i, b * TOK + 16 * c : b * TOK + 16 * c + 16, :] for c in range(8)]
                gls[s][b * BLOCK + TOK : b * BLOCK + BLOCK, :] = jnp.concatenate(parts, axis=1).astype(BF)


def attention(sc, msgs, lats, w_all):
    def whole(shape):
        return pl.BlockSpec(shape, lambda k, sc: (0,) * len(shape))

    slab = whole((SLAB, LATENT))
    in_specs = [whole((4, 2 * TOK + 16, MSG))] * 2 + [slab] * 4 + [whole((512, 512))] * 4
    args = [*msgs, *lats, *w_all]
    out_specs = [pl.BlockSpec((TOK, PAIR), lambda k, sc: (k, 0))] * 4
    out_shape = [jax.ShapeDtypeStruct((4 * TOK, PAIR), BF)] * 4
    out_specs += [slab] * 4 + [pl.BlockSpec((4, 1, 64, 512), lambda k, sc: (0, k, 0, 0))] * 2
    out_shape += [jax.ShapeDtypeStruct((SLAB, LATENT), BF)] * 4 + [jax.ShapeDtypeStruct((4, 4, 64, 512), BF)] * 2
    scratch = [
        pltpu.VMEM((4, 512, LATENT), BF),
        pltpu.VMEM((4, LATENT, 512), BF),
        pltpu.VMEM((4, 512, 128), BF),
        pltpu.VMEM((4, 128, 512), BF),
        pltpu.VMEM((4, 512, LATENT), F32),
        pltpu.VMEM((4, 512, ROPE), F32),
        pltpu.VMEM((512, 512), BF),
        pltpu.VMEM((512, 512), BF),
        pltpu.VMEM((2, 4, 512, 128), BF),
        pltpu.VMEM((2, 4, 512, 128), BF),
        pltpu.VMEM((2, 4, TOK, 256), BF),
        pltpu.VMEM((2, 4, TOK, VDIM), BF),
        pltpu.VMEM((2, 4, 8, TOK), F32),
        pltpu.VMEM((4, 512, 512), BF),
        pltpu.VMEM((4, TOK, PAIR), BF),
        pltpu.VMEM((512, 512), F32),
        pltpu.VMEM((512, 512), F32),
        pltpu.VMEM((512, 384), F32),
        pltpu.VMEM((512, 256), F32),
        pltpu.VMEM((512, 128), F32),
    ]
    outs = pl.pallas_call(
        attn_kernel,
        grid_spec=pltpu.PrefetchScalarGridSpec(
            num_scalar_prefetch=1, grid=(4,), in_specs=in_specs, out_specs=out_specs, scratch_shapes=scratch
        ),
        out_shape=out_shape,
        compiler_params=pltpu.CompilerParams(vmem_limit_bytes=56 * 1024 * 1024),
        cost_estimate=pl.CostEstimate(flops=50_000_000_000, bytes_accessed=14_000_000, transcendentals=5_400_000),
        name="attention",
    )(sc, *args)
    return outs[0:4], outs[4:8], outs[8], outs[9]


def unpack_kernel(sc, s0, s1, s2, s3, out):
    i = pl.program_id(0)
    for s, ref in enumerate((s0, s1, s2, s3)):

        @pl.when(((sc[3] - s) & 3) == i)
        def _():
            for kk, group in enumerate(GROUPS[0] + GROUPS[1]):
                lanes = pl.multiple_of(((sc[0] + group) & 3) * PAIR, 128)
                out[:, pl.ds(lanes, PAIR)] = ref[kk * TOK : kk * TOK + TOK, :]


def unpack(sc, pieces):
    spec = pl.BlockSpec(memory_space=pltpu.VMEM)
    return pl.pallas_call(
        unpack_kernel,
        grid=(4,),
        in_specs=[pl.BlockSpec(memory_space=pltpu.SMEM)] + [spec] * 4,
        out_specs=pl.BlockSpec((TOK, NZ * PAIR), lambda i: (0, i)),
        out_shape=jax.ShapeDtypeStruct((TOK, 16 * PAIR), BF),
        cost_estimate=pl.CostEstimate(flops=0, bytes_accessed=3_000_000, transcendentals=0),
        name="unpack",
    )(sc, *pieces)


def latents_kernel(b0, b1, b2, b3, out, out_rope):
    total = summed([b[...] for b in (b0, b1, b2, b3)])
    out[...] = total[:TOK]
    out_rope[...] = jnp.concatenate([total[TOK:, ROPE * c : ROPE * c + ROPE] for c in range(8)], axis=0).T


def finish_latents(pieces):
    spec = pl.BlockSpec(memory_space=pltpu.VMEM)
    return pl.pallas_call(
        latents_kernel,
        in_specs=[spec] * 4,
        out_specs=[spec] * 2,
        out_shape=[jax.ShapeDtypeStruct((TOK, LATENT), F32), jax.ShapeDtypeStruct((ROPE, TOK), F32)],
        cost_estimate=pl.CostEstimate(flops=20_000_000_000, bytes_accessed=1_000_000, transcendentals=0),
        name="finish_latents",
    )(*pieces)


def weights_kernel(sc, mine, other, out_k, out_v):
    core = sc[2]
    for base, ref in ((core, mine), (1 - core, other)):
        rows = pl.ds(pl.multiple_of(base * 256, 256), 256)
        for h in range(2):
            out_k[rows, h, :] = ref[:, h * 128 : h * 128 + 128].astype(F32)
            out_v[rows, h, :] = ref[:, 256 + h * 128 : 384 + h * 128].astype(F32)


def place_weights(sc, mine, other):
    spec = pl.BlockSpec(memory_space=pltpu.VMEM)
    return pl.pallas_call(
        weights_kernel,
        in_specs=[pl.BlockSpec(memory_space=pltpu.SMEM)] + [spec] * 2,
        out_specs=[spec] * 2,
        out_shape=[jax.ShapeDtypeStruct((512, 2, 128), F32)] * 2,
        cost_estimate=pl.CostEstimate(flops=0, bytes_accessed=2_000_000, transcendentals=0),
        name="place_weights",
    )(sc, mine, other)


def barrier(*values):
    return lax.optimization_barrier(values)


def summed(parts):
    total = parts[0].astype(F32)
    for n in range(1, len(parts)):
        total = total + parts[n].astype(F32)
    return total


def shards(query, latent, rope_key, grad_mantissa, grad_exponent, forward_out, offsets, w_key, w_value):
    dp, seq = lax.axis_index("dp"), lax.axis_index("seq")
    sc = jnp.stack([seq & 3, offsets[0], dp & 1, seq >> 2, dp >> 2]).astype(jnp.int32)

    ropes = rope_key[0].reshape(8, 16, ROPE).transpose(1, 0, 2).reshape(16, LATENT)
    own = jnp.concatenate([latent[0], ropes], axis=0)
    w_own = jnp.concatenate([w_key.reshape(LATENT, 256), w_value.reshape(LATENT, 256)], axis=1)
    near = [send(w_own, ring=-1), send(w_own, ring=1)]
    slab = jnp.concatenate([own] + [send(own, dz=s) for s in (1, 2, 3)], axis=0)

    inputs = (query[0], grad_mantissa[0], grad_exponent[0].T, forward_out[0])
    packed = pack(GROUPS[0], sc, *inputs)
    first = trade(packed, "x")
    slab, packed, *near = barrier(slab, packed, *near)
    lats = [slab] + [send(slab, dx=s) for s in (1, 2, 3)]

    first, w_held, packed = barrier(first, w_own, pack(GROUPS[1], sc, *inputs))
    far = jnp.concatenate([send(w_held[:256], ring=-2), send(w_held[256:], ring=2)], axis=0)
    second = trade(packed, "x")
    w_all = [w_own, near[0], far, near[1]]

    w_all = [w_all[k] for k in GROUPS[0] + GROUPS[1]]
    dqs, priors, keep, away = attention(sc, (first, second), lats, w_all)

    along_x = summed([priors[0]] + [send(priors[s], dx=s) for s in (1, 2, 3)]).astype(BF)
    blocks = along_x.reshape(NZ, BLOCK, LATENT)
    grad_latent, grad_rope = finish_latents([blocks[0]] + [send(blocks[s], dz=-s) for s in (1, 2, 3)])

    both = (keep.astype(F32) + send(away, dc=1).astype(F32)).astype(BF)
    partial = summed([both[0]] + [send(both[s], dy=s) for s in (1, 2, 3)]).astype(BF)
    by_group = {k: partial[n] for n, k in enumerate(GROUPS[0] + GROUPS[1])}
    own_heads = summed([by_group[0]] + [send(by_group[k], ring=(0, 1, 2, -1)[k]) for k in (1, 2, 3)]).astype(BF)
    grad_query = unpack(sc, [dqs[0]] + [send(dqs[s], dx=s) for s in (1, 2, 3)])
    own_heads = (own_heads.astype(F32) + send(own_heads, ring=4).astype(F32)).astype(BF)
    mine = spread(own_heads, "y").reshape(256, 512)
    total_key, total_value = place_weights(sc, mine, send(mine, dc=1))
    return grad_query[None], grad_latent[None], grad_rope.T[None], total_key, total_value


def solution(mesh):
    tokens = P("dp", "seq", None)
    heads = P(None, "seq", None)
    in_specs = (tokens,) * 6 + (P("dp"), heads, heads)
    out_specs = (tokens,) * 3 + (heads, heads)
    return jax.shard_map(shards, mesh=mesh, in_specs=in_specs, out_specs=out_specs, check_vma=False)
```
